32 devices in a mesh: dp: 8 (over y, x, core), seq: 4 (over z).
Axes of the slice: x: 2, y: 2, z: 4, core: 2. Of those that a mesh axis runs over, the one named last changes fastest.
Arguments:
- queries: bfloat16 [8, 512, 4096], P('dp', 'seq'), may hold values from -512 to 512
- key_rows: bfloat16 [8, 512, 4096], P('dp', 'seq'), may hold values from -18 to 18
- value_rows: bfloat16 [8, 512, 4096], P('dp', 'seq'), may hold values from -6 to 6
- w_out: bfloat16 [4096, 3072], P('seq', 'dp'), may hold values from -1.5 to 1.5
Outputs:
- attn_output: bfloat16 [8, 512, 3072], P('dp', 'seq')
The draws below stay inside these ranges and needn't reach their ends.
All inputs are finite; a program needn't handle non-finite values.
Results may differ from the reference program's by a relative error of at most 0.0095.
Values may be sent and summed in bfloat16 or wider, within the bound.
A program may use at most 128 MiB of HBM per device.

```python
import jax
import jax.numpy as jnp
from jax import lax

HEADS = 32
HEAD_DIM = 128
DOUT = 3072
LEN = 512
CLIPS = 8
N_SEQ = 4


def draw_pair(key):
    base = jax.random.fold_in(key, 7)
    key_query, key_keys = jax.random.split(base, 2)
    width = HEADS * HEAD_DIM
    queries = jax.random.truncated_normal(key_query, -6.0, 6.0, (CLIPS, LEN, width), jnp.float32)
    keys_all = jax.random.truncated_normal(key_keys, -6.0, 6.0, (CLIPS, LEN, width), jnp.float32)
    return (queries, keys_all)


def draw_queries(key, part):
    return draw_pair(key)[0].astype(jnp.bfloat16)


def draw_key_rows(key, part):
    return draw_pair(key)[1].astype(jnp.bfloat16)


def level_of(own_key, shape, cuts, smallest, high):
    factor_of = 1.0
    for dim, parts in cuts:
        draws = jax.random.uniform(jax.random.fold_in(jax.random.fold_in(own_key, 6), dim), (parts,), jnp.float32, smallest / len(cuts), high / len(cuts))
        factor_of = factor_of * jnp.repeat(jnp.exp(draws), shape[dim] // parts).reshape((-1,) + (1,) * (len(shape) - 1 - dim))
    return factor_of


def noise(key, extent, scale, reach, shards=(), dtype=jnp.bfloat16):
    level = level_of(key, extent, shards, -0.22, 0.18) if shards else 1.0
    drawn = jax.random.normal(key, extent, jnp.float32) * scale * level
    return jnp.minimum(jnp.maximum(drawn, -reach), reach).astype(dtype)


def setup_inputs(seed: int = 0) -> dict:
    key_of = jax.random.split(jax.random.key(seed), 5)
    return {
        "queries": draw_queries(jax.random.fold_in(key_of[4], 71), 0),
        "key_rows": draw_key_rows(jax.random.fold_in(key_of[4], 71), 0),
        "value_rows": noise(key_of[2], (CLIPS, LEN, HEADS * HEAD_DIM), 1.0, 6.0, ((0, 8), (1, 4))),
        "w_out": noise(key_of[3], (HEADS * HEAD_DIM, DOUT), (max(HEADS * HEAD_DIM // 256, 1)) ** -0.5, 1.5, ((0, 4), (1, 8))),
    }


def attend_block(qblock, keys_all, values_all, factor):
    scores = jnp.einsum("qhd,khd->hqk", qblock, keys_all) * factor
    largest = jnp.max(scores, axis=2, keepdims=True)
    weights = jnp.exp(scores - largest)
    totals = jnp.sum(weights, axis=2, keepdims=True)
    probs = (weights / totals).astype(jnp.bfloat16)
    probs = lax.optimization_barrier(probs).astype(jnp.float32)
    mixed = jnp.einsum("hqk,khd->qhd", probs, values_all)
    return mixed.astype(jnp.bfloat16)


def one_clip(triple, w_out):
    queries, keys_all, values_all = triple
    length = queries.shape[0]
    width = queries.shape[1]
    heads = width // HEAD_DIM
    block = min(512, length)
    factor = HEAD_DIM ** -0.5
    blocked = queries.astype(jnp.float32).reshape(length // block, block, heads, HEAD_DIM)
    keys_all = keys_all.astype(jnp.float32).reshape(length, heads, HEAD_DIM)
    values_all = values_all.astype(jnp.float32).reshape(length, heads, HEAD_DIM)
    outcome = lax.map(lambda qblock: attend_block(qblock, keys_all, values_all, factor), blocked)
    grouped = outcome.astype(jnp.float32).reshape(length, N_SEQ, width // N_SEQ)
    weight_groups = w_out.astype(jnp.float32).reshape(N_SEQ, width // N_SEQ, w_out.shape[1])
    group_part = jnp.einsum("tgk,gkc->gtc", grouped, weight_groups).astype(jnp.bfloat16)
    group_part = lax.optimization_barrier(group_part).astype(jnp.float32)
    return jnp.sum(group_part, axis=0).astype(jnp.bfloat16)


def reference(queries, key_rows, value_rows, w_out):
    return lax.map(lambda triple: one_clip(triple, w_out), (queries, key_rows, value_rows))
```

```python
import functools
import math

import jax
import jax.numpy as jnp
from jax import lax
from jax.experimental import pallas as pl
from jax.experimental.pallas import tpu as pltpu
from jax.sharding import PartitionSpec as P

HEAD_DIM = 128


def kernel(n, m, q_in, k_in, v_in, w_in, out, qb, kb, vb, wb, att, part, inbox,
           own_sem, qkv_send, qkv_recv, w_send, w_recv, sum_send, sum_recv):
    me = lax.axis_index("seq")
    col = lax.axis_index("dp")
    tokens = q_in.shape[0]
    feats = q_in.shape[1] // n
    heads = feats // HEAD_DIM
    length = tokens * n
    wcols = w_in.shape[1]

    def seq_peer(off):
        return lax.rem(me + off, n)

    def dp_peer(off):
        return lax.rem(col + off, m)

    barrier = pltpu.get_barrier_semaphore()
    for off in range(1, n):
        pl.semaphore_signal(barrier, inc=1, device_id={"seq": seq_peer(off)},
                            device_id_type=pl.DeviceIdType.MESH)
    for off in range(1, m):
        pl.semaphore_signal(barrier, inc=1, device_id={"dp": dp_peer(off)},
                            device_id_type=pl.DeviceIdType.MESH)
    pl.semaphore_wait(barrier, n + m - 2)

    trio = ((k_in, kb), (v_in, vb), (q_in, qb))

    def rows(dev):
        return pl.ds(pl.multiple_of(dev * tokens, tokens), tokens)

    def cols(dev):
        return pl.ds(pl.multiple_of(dev * feats, feats), feats)

    def qkv_copy(t, off):
        src, dst = trio[t]
        return pltpu.make_async_remote_copy(
            src_ref=src.at[:, cols(seq_peer(off))], dst_ref=dst.at[rows(me)],
            send_sem=qkv_send.at[t, off], recv_sem=qkv_recv.at[t, off],
            device_id={"seq": seq_peer(off)}, device_id_type=pl.DeviceIdType.MESH)

    def qkv_arrival(t, off):
        src, dst = trio[t]
        return pltpu.make_async_remote_copy(
            src_ref=src.at[:, cols(me)], dst_ref=dst.at[rows(lax.rem(me + n - off, n))],
            send_sem=qkv_send.at[t, off], recv_sem=qkv_recv.at[t, off],
            device_id={"seq": seq_peer(1)}, device_id_type=pl.DeviceIdType.MESH)

    def w_copy(off):
        return pltpu.make_async_remote_copy(
            src_ref=w_in, dst_ref=wb.at[col],
            send_sem=w_send.at[off], recv_sem=w_recv.at[off],
            device_id={"dp": dp_peer(off)}, device_id_type=pl.DeviceIdType.MESH)

    def w_arrival(off):
        return pltpu.make_async_remote_copy(
            src_ref=w_in, dst_ref=wb.at[lax.rem(col + m - off, m)],
            send_sem=w_send.at[off], recv_sem=w_recv.at[off],
            device_id={"dp": dp_peer(1)}, device_id_type=pl.DeviceIdType.MESH)

    for t in range(3):
        for off in range(1, n):
            qkv_copy(t, off).start()
    for off in range(1, m):
        w_copy(off).start()
    own = [pltpu.make_async_copy(trio[t][0].at[:, cols(me)], trio[t][1].at[rows(me)], own_sem.at[t])
           for t in range(3)]
    own.append(pltpu.make_async_copy(w_in, wb.at[col], own_sem.at[3]))
    for copy in own:
        copy.start()
    for copy in own:
        copy.wait()
    for t in range(2):
        for off in range(1, n):
            qkv_arrival(t, off).wait_recv()

    scale = HEAD_DIM ** -0.5 * math.log2(math.e)

    def attend(dest):
        for h in range(heads):
            c = slice(h * HEAD_DIM, (h + 1) * HEAD_DIM)
            s = lax.dot_general(qb[rows(dest), c], kb[:, c], (((1,), (1,)), ((), ())),
                                preferred_element_type=jnp.float32)
            top = jnp.max(s, axis=1, keepdims=True)
            p = jnp.exp2((s - top) * scale)
            total = jnp.sum(p, axis=1, keepdims=True)
            o = jnp.dot(p.astype(jnp.bfloat16), vb[:, c], preferred_element_type=jnp.float32)
            att[:, c] = (o / total).astype(jnp.bfloat16)

    def project(dest):
        for j in range(m):
            part[dest, :, j * wcols:(j + 1) * wcols] = jnp.dot(
                att[...], wb[j], preferred_element_type=jnp.float32).astype(jnp.bfloat16)

    def sum_copy(dest, up):
        target = me + 2 * up - 1
        slot = jnp.where((up == 0) & (target == dest), n, dest)
        return pltpu.make_async_remote_copy(
            src_ref=part.at[dest], dst_ref=inbox.at[slot],
            send_sem=sum_send.at[dest], recv_sem=sum_recv.at[slot],
            device_id={"seq": target}, device_id_type=pl.DeviceIdType.MESH)

    def sum_arrival(slot):
        return pltpu.make_async_remote_copy(
            src_ref=part.at[0], dst_ref=inbox.at[slot],
            send_sem=sum_send.at[0], recv_sem=sum_recv.at[slot],
            device_id={"seq": seq_peer(1)}, device_id_type=pl.DeviceIdType.MESH)

    low = jnp.where(me < n // 2, 1, 0)

    def item(index, carry):
        s = index // 2
        pos = index % 2
        up = jnp.where(pos == 0, low, 1 - low)
        dest = jnp.where(up == 1, n - 1 - s, s)

        @pl.when(s < (n + 1) // 2)
        def _():
            @pl.when(dest != me)
            def _():
                qkv_arrival(2, lax.rem(me - dest + n, n)).wait_recv()

            attend(dest)

            @pl.when(index == 0)
            def _():
                for off in range(1, m):
                    w_arrival(off).wait_recv()

            project(dest)

        active = jnp.where(up == 1, jnp.where(me < dest, 1, 0), jnp.where(me > dest, 1, 0))
        inner = jnp.where(up == 1, jnp.where(me > 0, 1, 0), jnp.where(me < n - 1, 1, 0))

        @pl.when(active == 1)
        def _():
            @pl.when(inner == 1)
            def _():
                sum_arrival(dest).wait_recv()
                part[dest] = (part[dest].astype(jnp.float32)
                              + inbox[dest].astype(jnp.float32)).astype(jnp.bfloat16)

            sum_copy(dest, up).start()

        return carry

    lax.fori_loop(0, 2 * n, item, 0)

    @pl.when(me > 0)
    def _():
        sum_arrival(me).wait_recv()

    @pl.when(me < n - 1)
    def _():
        sum_arrival(n).wait_recv()

    @pl.when(me == 0)
    def _():
        out[...] = (part[me].astype(jnp.float32) + inbox[n].astype(jnp.float32)).astype(jnp.bfloat16)

    @pl.when(me == n - 1)
    def _():
        out[...] = (part[me].astype(jnp.float32) + inbox[me].astype(jnp.float32)).astype(jnp.bfloat16)

    @pl.when((me > 0) & (me < n - 1))
    def _():
        out[...] = (part[me].astype(jnp.float32) + inbox[me].astype(jnp.float32)
                    + inbox[n].astype(jnp.float32)).astype(jnp.bfloat16)

    for t in range(3):
        for off in range(1, n):
            qkv_copy(t, off).wait_send()
    for off in range(1, m):
        w_copy(off).wait_send()

    def drain(dest, carry):
        @pl.when(dest != me)
        def _():
            sum_copy(dest, jnp.where(dest > me, 1, 0)).wait_send()
        return carry

    lax.fori_loop(0, n, drain, 0)


def per_device(n, m, queries, key_rows, value_rows, w_out):
    tokens, width = queries.shape[1:]
    depth, wcols = w_out.shape
    feats = width // n
    length = tokens * n
    dout = wcols * m
    bf16 = jnp.bfloat16
    vmem = pltpu.VMEM
    dma = pltpu.SemaphoreType.DMA
    flat = [a.reshape(tokens, width) for a in (queries, key_rows, value_rows)]
    result = pl.pallas_call(
        functools.partial(kernel, n, m),
        out_shape=jax.ShapeDtypeStruct((tokens, dout), bf16),
        in_specs=[pl.BlockSpec(memory_space=pl.ANY)] * 4,
        out_specs=pl.BlockSpec(memory_space=vmem),
        scratch_shapes=[
            vmem((length, feats), bf16), vmem((length, feats), bf16), vmem((length, feats), bf16),
            vmem((m, depth, wcols), bf16), vmem((tokens, feats), bf16),
            vmem((n, tokens, dout), bf16), vmem((n + 1, tokens, dout), bf16),
            dma((4,)), dma((3, n)), dma((3, n)), dma((m,)), dma((m,)), dma((n,)), dma((n + 1,)),
        ],
        compiler_params=pltpu.CompilerParams(
            collective_id=0, has_side_effects=True, vmem_limit_bytes=56 * 1024 * 1024),
        cost_estimate=pl.CostEstimate(
            flops=4 * length * length * feats + 2 * length * feats * dout,
            bytes_accessed=2 * (3 * tokens * width + depth * wcols),
            transcendentals=length * length * feats // HEAD_DIM),
    )(*flat, w_out)
    return result.reshape(1, tokens, dout)


def solution(mesh):
    n, m = mesh.shape["seq"], mesh.shape["dp"]
    in_specs = (P("dp", "seq", None), P("dp", "seq", None), P("dp", "seq", None), P("seq", "dp"))
    out_specs = P("dp", "seq", None)
    return jax.shard_map(
        functools.partial(per_device, n, m), mesh=mesh, in_specs=in_specs, out_specs=out_specs,
        check_vma=False
    )
```

```python
import functools
import math

import jax
import jax.numpy as jnp
from jax import lax
from jax.experimental import pallas as pl
from jax.experimental.pallas import tpu as pltpu
from jax.sharding import PartitionSpec as P

HEAD_DIM = 128


def kernel(n, m, q_in, k_in, v_in, w_in, out, qb, kb, vb, wb, att, part, inbox,
           own_sem, qkv_send, qkv_recv, w_send, w_recv, sum_send, sum_recv):
    me = lax.axis_index("seq")
    col = lax.axis_index("dp")
    tokens = q_in.shape[0]
    feats = q_in.shape[1] // n
    heads = feats // HEAD_DIM
    length = tokens * n
    wcols = w_in.shape[1]

    def seq_peer(off):
        return lax.rem(me + off, n)

    chips = m // 2
    sibling = col + 1 - 2 * lax.rem(col, 2)

    def w_peer(chip):
        return lax.rem(col + 2 * chip, m) if chip else sibling

    def w_origin(chip):
        return lax.rem(col + m - 2 * chip, m) if chip else sibling

    barrier = pltpu.get_barrier_semaphore()
    for off in range(1, n):
        pl.semaphore_signal(barrier, inc=1, device_id={"seq": seq_peer(off)},
                            device_id_type=pl.DeviceIdType.MESH)
    for chip in range(chips):
        pl.semaphore_signal(barrier, inc=1, device_id={"dp": w_peer(chip)},
                            device_id_type=pl.DeviceIdType.MESH)
    pl.semaphore_wait(barrier, n - 1 + chips)

    trio = ((k_in, kb), (v_in, vb), (q_in, qb))

    def rows(dev):
        return pl.ds(pl.multiple_of(dev * tokens, tokens), tokens)

    def cols(dev):
        return pl.ds(pl.multiple_of(dev * feats, feats), feats)

    def qkv_copy(t, off):
        src, dst = trio[t]
        return pltpu.make_async_remote_copy(
            src_ref=src.at[:, cols(seq_peer(off))], dst_ref=dst.at[rows(me)],
            send_sem=qkv_send.at[t, off], recv_sem=qkv_recv.at[t, off],
            device_id={"seq": seq_peer(off)}, device_id_type=pl.DeviceIdType.MESH)

    def qkv_arrival(t, off):
        src, dst = trio[t]
        return pltpu.make_async_remote_copy(
            src_ref=src.at[:, cols(me)], dst_ref=dst.at[rows(lax.rem(me + n - off, n))],
            send_sem=qkv_send.at[t, off], recv_sem=qkv_recv.at[t, off],
            device_id={"seq": seq_peer(1)}, device_id_type=pl.DeviceIdType.MESH)

    def w_copy(chip):
        return pltpu.make_async_remote_copy(
            src_ref=w_in, dst_ref=wb.at[col],
            send_sem=w_send.at[chip], recv_sem=w_recv.at[chip],
            device_id={"dp": w_peer(chip)}, device_id_type=pl.DeviceIdType.MESH)

    def w_arrival(chip):
        return pltpu.make_async_remote_copy(
            src_ref=w_in, dst_ref=wb.at[w_origin(chip)],
            send_sem=w_send.at[chip], recv_sem=w_recv.at[chip],
            device_id={"dp": sibling}, device_id_type=pl.DeviceIdType.MESH)

    def w_pass(chip):
        return pltpu.make_async_remote_copy(
            src_ref=wb.at[w_origin(chip)], dst_ref=wb.at[w_origin(chip)],
            send_sem=w_send.at[chips + chip], recv_sem=w_recv.at[chips + chip],
            device_id={"dp": sibling}, device_id_type=pl.DeviceIdType.MESH)

    def w_passed(chip):
        origin = lax.rem(sibling + m - 2 * chip, m)
        return pltpu.make_async_remote_copy(
            src_ref=w_in, dst_ref=wb.at[origin],
            send_sem=w_send.at[chips + chip], recv_sem=w_recv.at[chips + chip],
            device_id={"dp": sibling}, device_id_type=pl.DeviceIdType.MESH)

    low = jnp.where(me < n // 2, 1, 0)

    def send_queries():
        for i in range(n):
            target = jnp.where(low == 1, n - 1 - i, i)

            @pl.when(target != me)
            def _():
                qkv_copy(2, lax.rem(target - me + n, n)).start()

    for t in range(2):
        for off in range(1, n):
            qkv_copy(t, off).start()
    for chip in range(1, chips):
        w_copy(chip).start()
    w_copy(0).start()
    own = [pltpu.make_async_copy(trio[t][0].at[:, cols(me)], trio[t][1].at[rows(me)], own_sem.at[t])
           for t in range(3)]
    own.append(pltpu.make_async_copy(w_in, wb.at[col], own_sem.at[3]))
    for copy in own:
        copy.start()
    for copy in own:
        copy.wait()
    for off in range(1, n):
        qkv_arrival(0, off).wait_recv()
    send_queries()
    for chip in range(1, chips):
        w_arrival(chip).wait_recv()
        w_pass(chip).start()
    for off in range(1, n):
        qkv_arrival(1, off).wait_recv()

    scale = HEAD_DIM ** -0.5 * math.log2(math.e)

    def attend(dest):
        for h in range(heads):
            c = slice(h * HEAD_DIM, (h + 1) * HEAD_DIM)
            s = lax.dot_general(qb[rows(dest), c], kb[:, c], (((1,), (1,)), ((), ())),
                                preferred_element_type=jnp.float32)
            top = jnp.max(s, axis=1, keepdims=True)
            p = jnp.exp2((s - top) * scale)
            total = jnp.sum(p, axis=1, keepdims=True)
            o = jnp.dot(p.astype(jnp.bfloat16), vb[:, c], preferred_element_type=jnp.float32)
            att[:, c] = (o / total).astype(jnp.bfloat16)

    def project(dest):
        for j in range(m):
            part[dest, :, j * wcols:(j + 1) * wcols] = jnp.dot(
                att[...], wb[j], preferred_element_type=jnp.float32).astype(jnp.bfloat16)

    def sum_copy(dest, up):
        target = me + 2 * up - 1
        slot = jnp.where((up == 0) & (target == dest), n, dest)
        return pltpu.make_async_remote_copy(
            src_ref=part.at[dest], dst_ref=inbox.at[slot],
            send_sem=sum_send.at[dest], recv_sem=sum_recv.at[slot],
            device_id={"seq": target}, device_id_type=pl.DeviceIdType.MESH)

    def sum_arrival(slot):
        return pltpu.make_async_remote_copy(
            src_ref=part.at[0], dst_ref=inbox.at[slot],
            send_sem=sum_send.at[0], recv_sem=sum_recv.at[slot],
            device_id={"seq": seq_peer(1)}, device_id_type=pl.DeviceIdType.MESH)

    def item(index, carry):
        s = index // 2
        pos = index % 2
        up = jnp.where(pos == 0, low, 1 - low)
        dest = jnp.where(up == 1, n - 1 - s, s)

        @pl.when(s < (n + 1) // 2)
        def _():
            @pl.when(dest != me)
            def _():
                qkv_arrival(2, lax.rem(me - dest + n, n)).wait_recv()

            attend(dest)

            @pl.when(index == 0)
            def _():
                w_arrival(0).wait_recv()
                for chip in range(1, chips):
                    w_passed(chip).wait_recv()

            project(dest)

        active = jnp.where(up == 1, jnp.where(me < dest, 1, 0), jnp.where(me > dest, 1, 0))
        inner = jnp.where(up == 1, jnp.where(me > 0, 1, 0), jnp.where(me < n - 1, 1, 0))

        @pl.when(active == 1)
        def _():
            @pl.when(inner == 1)
            def _():
                sum_arrival(dest).wait_recv()
                part[dest] = (part[dest].astype(jnp.float32)
                              + inbox[dest].astype(jnp.float32)).astype(jnp.bfloat16)

            sum_copy(dest, up).start()

        return carry

    lax.fori_loop(0, 2 * n, item, 0)

    @pl.when(me > 0)
    def _():
        sum_arrival(me).wait_recv()

    @pl.when(me < n - 1)
    def _():
        sum_arrival(n).wait_recv()

    @pl.when(me == 0)
    def _():
        out[...] = (part[me].astype(jnp.float32) + inbox[n].astype(jnp.float32)).astype(jnp.bfloat16)

    @pl.when(me == n - 1)
    def _():
        out[...] = (part[me].astype(jnp.float32) + inbox[me].astype(jnp.float32)).astype(jnp.bfloat16)

    @pl.when((me > 0) & (me < n - 1))
    def _():
        out[...] = (part[me].astype(jnp.float32) + inbox[me].astype(jnp.float32)
                    + inbox[n].astype(jnp.float32)).astype(jnp.bfloat16)

    for t in range(3):
        for off in range(1, n):
            qkv_copy(t, off).wait_send()
    for chip in range(chips):
        w_copy(chip).wait_send()
    for chip in range(1, chips):
        w_pass(chip).wait_send()

    def drain(dest, carry):
        @pl.when(dest != me)
        def _():
            sum_copy(dest, jnp.where(dest > me, 1, 0)).wait_send()
        return carry

    lax.fori_loop(0, n, drain, 0)


def per_device(n, m, queries, key_rows, value_rows, w_out):
    tokens, width = queries.shape[1:]
    depth, wcols = w_out.shape
    feats = width // n
    length = tokens * n
    dout = wcols * m
    bf16 = jnp.bfloat16
    vmem = pltpu.VMEM
    dma = pltpu.SemaphoreType.DMA
    flat = [a.reshape(tokens, width) for a in (queries, key_rows, value_rows)]
    result = pl.pallas_call(
        functools.partial(kernel, n, m),
        out_shape=jax.ShapeDtypeStruct((tokens, dout), bf16),
        in_specs=[pl.BlockSpec(memory_space=pl.ANY)] * 4,
        out_specs=pl.BlockSpec(memory_space=vmem),
        scratch_shapes=[
            vmem((length, feats), bf16), vmem((length, feats), bf16), vmem((length, feats), bf16),
            vmem((m, depth, wcols), bf16), vmem((tokens, feats), bf16),
            vmem((n, tokens, dout), bf16), vmem((n + 1, tokens, dout), bf16),
            dma((4,)), dma((3, n)), dma((3, n)), dma((m,)), dma((m,)), dma((n,)), dma((n + 1,)),
        ],
        compiler_params=pltpu.CompilerParams(
            collective_id=0, has_side_effects=True, vmem_limit_bytes=56 * 1024 * 1024),
        cost_estimate=pl.CostEstimate(
            flops=4 * length * length * feats + 2 * length * feats * dout,
            bytes_accessed=2 * (3 * tokens * width + depth * wcols),
            transcendentals=length * length * feats // HEAD_DIM),
    )(*flat, w_out)
    return result.reshape(1, tokens, dout)


def solution(mesh):
    n, m = mesh.shape["seq"], mesh.shape["dp"]
    in_specs = (P("dp", "seq", None), P("dp", "seq", None), P("dp", "seq", None), P("seq", "dp"))
    out_specs = P("dp", "seq", None)
    return jax.shard_map(
        functools.partial(per_device, n, m), mesh=mesh, in_specs=in_specs, out_specs=out_specs,
        check_vma=False
    )
```

```python
import functools
import math

import jax
import jax.numpy as jnp
from jax import lax
from jax.experimental import pallas as pl
from jax.experimental.pallas import tpu as pltpu
from jax.sharding import PartitionSpec as P

HEAD_DIM = 128


def kernel(n, m, q_in, k_in, v_in, w_in, out, qb, kb, vb, wb, att, part, inbox,
           own_sem, qkv_send, qkv_recv, w_send, w_recv, sum_send, sum_recv):
    me = lax.axis_index("seq")
    col = lax.axis_index("dp")
    tokens = q_in.shape[0]
    feats = q_in.shape[1] // n
    heads = feats // HEAD_DIM
    length = tokens * n
    wcols = w_in.shape[1]

    def seq_peer(off):
        return lax.rem(me + off, n)

    chips = m // 2
    sibling = col + 1 - 2 * lax.rem(col, 2)

    def w_peer(chip):
        return lax.rem(col + 2 * chip, m) if chip else sibling

    def w_origin(chip):
        return lax.rem(col + m - 2 * chip, m) if chip else sibling

    barrier = pltpu.get_barrier_semaphore()
    for off in range(1, n):
        pl.semaphore_signal(barrier, inc=1, device_id={"seq": seq_peer(off)},
                            device_id_type=pl.DeviceIdType.MESH)
    for chip in range(chips):
        pl.semaphore_signal(barrier, inc=1, device_id={"dp": w_peer(chip)},
                            device_id_type=pl.DeviceIdType.MESH)
    pl.semaphore_wait(barrier, n - 1 + chips)

    trio = ((k_in, kb), (v_in, vb), (q_in, qb))

    def rows(dev):
        return pl.ds(pl.multiple_of(dev * tokens, tokens), tokens)

    def cols(dev):
        return pl.ds(pl.multiple_of(dev * feats, feats), feats)

    def qkv_copy(t, off):
        src, dst = trio[t]
        return pltpu.make_async_remote_copy(
            src_ref=src.at[:, cols(seq_peer(off))], dst_ref=dst.at[rows(me)],
            send_sem=qkv_send.at[t, off], recv_sem=qkv_recv.at[t, off],
            device_id={"seq": seq_peer(off)}, device_id_type=pl.DeviceIdType.MESH)

    def qkv_arrival(t, off):
        src, dst = trio[t]
        return pltpu.make_async_remote_copy(
            src_ref=src.at[:, cols(me)], dst_ref=dst.at[rows(lax.rem(me + n - off, n))],
            send_sem=qkv_send.at[t, off], recv_sem=qkv_recv.at[t, off],
            device_id={"seq": seq_peer(1)}, device_id_type=pl.DeviceIdType.MESH)

    def w_copy(chip):
        return pltpu.make_async_remote_copy(
            src_ref=w_in, dst_ref=wb.at[col],
            send_sem=w_send.at[chip], recv_sem=w_recv.at[chip],
            device_id={"dp": w_peer(chip)}, device_id_type=pl.DeviceIdType.MESH)

    def w_arrival(chip):
        return pltpu.make_async_remote_copy(
            src_ref=w_in, dst_ref=wb.at[w_origin(chip)],
            send_sem=w_send.at[chip], recv_sem=w_recv.at[chip],
            device_id={"dp": sibling}, device_id_type=pl.DeviceIdType.MESH)

    def w_pass(chip):
        return pltpu.make_async_remote_copy(
            src_ref=wb.at[w_origin(chip)], dst_ref=wb.at[w_origin(chip)],
            send_sem=w_send.at[chips + chip], recv_sem=w_recv.at[chips + chip],
            device_id={"dp": sibling}, device_id_type=pl.DeviceIdType.MESH)

    def w_passed(chip):
        origin = lax.rem(sibling + m - 2 * chip, m)
        return pltpu.make_async_remote_copy(
            src_ref=w_in, dst_ref=wb.at[origin],
            send_sem=w_send.at[chips + chip], recv_sem=w_recv.at[chips + chip],
            device_id={"dp": sibling}, device_id_type=pl.DeviceIdType.MESH)

    low = jnp.where(me < n // 2, 1, 0)

    for chip in range(1, chips):
        w_copy(chip).start()
    w_copy(0).start()
    for i in range(n):
        target = jnp.where(low == 1, n - 1 - i, i)

        @pl.when(target != me)
        def _():
            for t in range(3):
                qkv_copy(t, lax.rem(target - me + n, n)).start()
    own = [pltpu.make_async_copy(trio[t][0].at[:, cols(me)], trio[t][1].at[rows(me)], own_sem.at[t])
           for t in range(3)]
    own.append(pltpu.make_async_copy(w_in, wb.at[col], own_sem.at[3]))
    for copy in own:
        copy.start()
    for copy in own:
        copy.wait()
    for off in range(1, n):
        qkv_arrival(0, off).wait_recv()
    for chip in range(1, chips):
        w_arrival(chip).wait_recv()
        w_pass(chip).start()
    for off in range(1, n):
        qkv_arrival(1, off).wait_recv()

    scale = HEAD_DIM ** -0.5 * math.log2(math.e)

    def attend(dest):
        for h in range(heads):
            c = slice(h * HEAD_DIM, (h + 1) * HEAD_DIM)
            s = lax.dot_general(qb[rows(dest), c], kb[:, c], (((1,), (1,)), ((), ())),
                                preferred_element_type=jnp.float32)
            top = jnp.max(s, axis=1, keepdims=True)
            p = jnp.exp2((s - top) * scale)
            total = jnp.sum(p, axis=1, keepdims=True)
            o = jnp.dot(p.astype(jnp.bfloat16), vb[:, c], preferred_element_type=jnp.float32)
            att[:, c] = (o / total).astype(jnp.bfloat16)

    def project(dest):
        for j in range(m):
            part[dest, :, j * wcols:(j + 1) * wcols] = jnp.dot(
                att[...], wb[j], preferred_element_type=jnp.float32).astype(jnp.bfloat16)

    def sum_copy(dest, up):
        target = me + 2 * up - 1
        slot = jnp.where((up == 0) & (target == dest), n, dest)
        return pltpu.make_async_remote_copy(
            src_ref=part.at[dest], dst_ref=inbox.at[slot],
            send_sem=sum_send.at[dest], recv_sem=sum_recv.at[slot],
            device_id={"seq": target}, device_id_type=pl.DeviceIdType.MESH)

    def sum_arrival(slot):
        return pltpu.make_async_remote_copy(
            src_ref=part.at[0], dst_ref=inbox.at[slot],
            send_sem=sum_send.at[0], recv_sem=sum_recv.at[slot],
            device_id={"seq": seq_peer(1)}, device_id_type=pl.DeviceIdType.MESH)

    def item(index, carry):
        s = index // 2
        pos = index % 2
        up = jnp.where(pos == 0, low, 1 - low)
        dest = jnp.where(up == 1, n - 1 - s, s)

        @pl.when(s < (n + 1) // 2)
        def _():
            @pl.when(dest != me)
            def _():
                qkv_arrival(2, lax.rem(me - dest + n, n)).wait_recv()

            attend(dest)

            @pl.when(index == 0)
            def _():
                w_arrival(0).wait_recv()
                for chip in range(1, chips):
                    w_passed(chip).wait_recv()

            project(dest)

        active = jnp.where(up == 1, jnp.where(me < dest, 1, 0), jnp.where(me > dest, 1, 0))
        inner = jnp.where(up == 1, jnp.where(me > 0, 1, 0), jnp.where(me < n - 1, 1, 0))

        @pl.when(active == 1)
        def _():
            @pl.when(inner == 1)
            def _():
                sum_arrival(dest).wait_recv()
                part[dest] = (part[dest].astype(jnp.float32)
                              + inbox[dest].astype(jnp.float32)).astype(jnp.bfloat16)

            sum_copy(dest, up).start()

        return carry

    lax.fori_loop(0, 2 * n, item, 0)

    @pl.when(me > 0)
    def _():
        sum_arrival(me).wait_recv()

    @pl.when(me < n - 1)
    def _():
        sum_arrival(n).wait_recv()

    @pl.when(me == 0)
    def _():
        out[...] = (part[me].astype(jnp.float32) + inbox[n].astype(jnp.float32)).astype(jnp.bfloat16)

    @pl.when(me == n - 1)
    def _():
        out[...] = (part[me].astype(jnp.float32) + inbox[me].astype(jnp.float32)).astype(jnp.bfloat16)

    @pl.when((me > 0) & (me < n - 1))
    def _():
        out[...] = (part[me].astype(jnp.float32) + inbox[me].astype(jnp.float32)
                    + inbox[n].astype(jnp.float32)).astype(jnp.bfloat16)

    for t in range(3):
        for off in range(1, n):
            qkv_copy(t, off).wait_send()
    for chip in range(chips):
        w_copy(chip).wait_send()
    for chip in range(1, chips):
        w_pass(chip).wait_send()

    def drain(dest, carry):
        @pl.when(dest != me)
        def _():
            sum_copy(dest, jnp.where(dest > me, 1, 0)).wait_send()
        return carry

    lax.fori_loop(0, n, drain, 0)


def per_device(n, m, queries, key_rows, value_rows, w_out):
    tokens, width = queries.shape[1:]
    depth, wcols = w_out.shape
    feats = width // n
    length = tokens * n
    dout = wcols * m
    bf16 = jnp.bfloat16
    vmem = pltpu.VMEM
    dma = pltpu.SemaphoreType.DMA
    flat = [a.reshape(tokens, width) for a in (queries, key_rows, value_rows)]
    result = pl.pallas_call(
        functools.partial(kernel, n, m),
        out_shape=jax.ShapeDtypeStruct((tokens, dout), bf16),
        in_specs=[pl.BlockSpec(memory_space=pl.ANY)] * 4,
        out_specs=pl.BlockSpec(memory_space=vmem),
        scratch_shapes=[
            vmem((length, feats), bf16), vmem((length, feats), bf16), vmem((length, feats), bf16),
            vmem((m, depth, wcols), bf16), vmem((tokens, feats), bf16),
            vmem((n, tokens, dout), bf16), vmem((n + 1, tokens, dout), bf16),
            dma((4,)), dma((3, n)), dma((3, n)), dma((m,)), dma((m,)), dma((n,)), dma((n + 1,)),
        ],
        compiler_params=pltpu.CompilerParams(
            collective_id=0, has_side_effects=True, vmem_limit_bytes=56 * 1024 * 1024),
        cost_estimate=pl.CostEstimate(
            flops=4 * length * length * feats + 2 * length * feats * dout,
            bytes_accessed=2 * (3 * tokens * width + depth * wcols),
            transcendentals=length * length * feats // HEAD_DIM),
    )(*flat, w_out)
    return result.reshape(1, tokens, dout)


def solution(mesh):
    n, m = mesh.shape["seq"], mesh.shape["dp"]
    in_specs = (P("dp", "seq", None), P("dp", "seq", None), P("dp", "seq", None), P("seq", "dp"))
    out_specs = P("dp", "seq", None)
    return jax.shard_map(
        functools.partial(per_device, n, m), mesh=mesh, in_specs=in_specs, out_specs=out_specs,
        check_vma=False
    )
```

```python
import functools
import math

import jax
import jax.numpy as jnp
from jax import lax
from jax.experimental import pallas as pl
from jax.experimental.pallas import tpu as pltpu
from jax.sharding import PartitionSpec as P

HEAD_DIM = 128


def kernel(n, m, q_in, k_in, v_in, w_in, out, qb, kb, vb, wb, att, part, inbox,
           own_sem, qkv_send, qkv_recv, w_send, w_recv, sum_send, sum_recv):
    me = lax.axis_index("seq")
    col = lax.axis_index("dp")
    tokens = q_in.shape[0]
    feats = q_in.shape[1] // n
    heads = feats // HEAD_DIM
    length = tokens * n
    wcols = w_in.shape[1]

    def seq_peer(off):
        return lax.rem(me + off, n)

    chips = m // 2
    sibling = col + 1 - 2 * lax.rem(col, 2)

    def w_peer(chip):
        return lax.rem(col + 2 * chip, m) if chip else sibling

    def w_origin(chip):
        return lax.rem(col + m - 2 * chip, m) if chip else sibling

    barrier = pltpu.get_barrier_semaphore()
    for off in range(1, n):
        pl.semaphore_signal(barrier, inc=1, device_id={"seq": seq_peer(off)},
                            device_id_type=pl.DeviceIdType.MESH)
    for chip in range(chips):
        pl.semaphore_signal(barrier, inc=1, device_id={"dp": w_peer(chip)},
                            device_id_type=pl.DeviceIdType.MESH)
    pl.semaphore_wait(barrier, n - 1 + chips)

    trio = ((k_in, kb), (v_in, vb), (q_in, qb))

    def rows(dev):
        return pl.ds(pl.multiple_of(dev * tokens, tokens), tokens)

    def cols(dev):
        return pl.ds(pl.multiple_of(dev * feats, feats), feats)

    def qkv_copy(t, off):
        src, dst = trio[t]
        return pltpu.make_async_remote_copy(
            src_ref=src.at[:, cols(seq_peer(off))], dst_ref=dst.at[rows(me)],
            send_sem=qkv_send.at[t, off], recv_sem=qkv_recv.at[t, off],
            device_id={"seq": seq_peer(off)}, device_id_type=pl.DeviceIdType.MESH)

    def qkv_arrival(t, off):
        src, dst = trio[t]
        return pltpu.make_async_remote_copy(
            src_ref=src.at[:, cols(me)], dst_ref=dst.at[rows(lax.rem(me + n - off, n))],
            send_sem=qkv_send.at[t, off], recv_sem=qkv_recv.at[t, off],
            device_id={"seq": seq_peer(1)}, device_id_type=pl.DeviceIdType.MESH)

    def w_copy(chip):
        return pltpu.make_async_remote_copy(
            src_ref=w_in, dst_ref=wb.at[col],
            send_sem=w_send.at[chip], recv_sem=w_recv.at[chip],
            device_id={"dp": w_peer(chip)}, device_id_type=pl.DeviceIdType.MESH)

    def w_arrival(chip):
        return pltpu.make_async_remote_copy(
            src_ref=w_in, dst_ref=wb.at[w_origin(chip)],
            send_sem=w_send.at[chip], recv_sem=w_recv.at[chip],
            device_id={"dp": sibling}, device_id_type=pl.DeviceIdType.MESH)

    def w_pass(chip):
        return pltpu.make_async_remote_copy(
            src_ref=wb.at[w_origin(chip)], dst_ref=wb.at[w_origin(chip)],
            send_sem=w_send.at[chips + chip], recv_sem=w_recv.at[chips + chip],
            device_id={"dp": sibling}, device_id_type=pl.DeviceIdType.MESH)

    def w_passed(chip):
        origin = lax.rem(sibling + m - 2 * chip, m)
        return pltpu.make_async_remote_copy(
            src_ref=w_in, dst_ref=wb.at[origin],
            send_sem=w_send.at[chips + chip], recv_sem=w_recv.at[chips + chip],
            device_id={"dp": sibling}, device_id_type=pl.DeviceIdType.MESH)

    low = jnp.where(me < n // 2, 1, 0)

    for chip in range(1, chips):
        w_copy(chip).start()
    w_copy(0).start()
    for i in range(n):
        target = jnp.where(low == 1, n - 1 - i, i)

        @pl.when(target != me)
        def _():
            for t in range(3):
                qkv_copy(t, lax.rem(target - me + n, n)).start()
    own = [pltpu.make_async_copy(trio[t][0].at[:, cols(me)], trio[t][1].at[rows(me)], own_sem.at[t])
           for t in range(3)]
    own.append(pltpu.make_async_copy(w_in, wb.at[col], own_sem.at[3]))
    for copy in own:
        copy.start()
    for copy in own:
        copy.wait()
    for off in range(1, n):
        qkv_arrival(0, off).wait_recv()
    for chip in range(1, chips):
        w_arrival(chip).wait_recv()
        w_pass(chip).start()
    for off in range(1, n):
        qkv_arrival(1, off).wait_recv()

    scale = HEAD_DIM ** -0.5 * math.log2(math.e)

    def attend(dest):
        for h in range(heads):
            c = slice(h * HEAD_DIM, (h + 1) * HEAD_DIM)
            s = lax.dot_general(qb[rows(dest), c], kb[:, c], (((1,), (1,)), ((), ())),
                                preferred_element_type=jnp.float32)
            top = jnp.max(s, axis=1, keepdims=True)
            p = jnp.exp2((s - top) * scale)
            total = jnp.sum(p, axis=1, keepdims=True)
            o = jnp.dot(p.astype(jnp.bfloat16), vb[:, c], preferred_element_type=jnp.float32)
            att[:, c] = (o / total).astype(jnp.bfloat16)

    half = m * wcols // 2

    def project(dest, c):
        for j in range(c * m // 2, (c + 1) * m // 2):
            part[dest, :, j * wcols:(j + 1) * wcols] = jnp.dot(
                att[...], wb[j], preferred_element_type=jnp.float32).astype(jnp.bfloat16)

    def sum_copy(dest, up, c):
        target = me + 2 * up - 1
        slot = jnp.where((up == 0) & (target == dest), n, dest)
        return pltpu.make_async_remote_copy(
            src_ref=part.at[dest, :, pl.ds(c * half, half)],
            dst_ref=inbox.at[slot, :, pl.ds(c * half, half)],
            send_sem=sum_send.at[dest, c], recv_sem=sum_recv.at[slot, c],
            device_id={"seq": target}, device_id_type=pl.DeviceIdType.MESH)

    def sum_arrival(slot, c):
        return pltpu.make_async_remote_copy(
            src_ref=part.at[0, :, pl.ds(c * half, half)],
            dst_ref=inbox.at[slot, :, pl.ds(c * half, half)],
            send_sem=sum_send.at[0, c], recv_sem=sum_recv.at[slot, c],
            device_id={"seq": seq_peer(1)}, device_id_type=pl.DeviceIdType.MESH)

    def item(index, carry):
        s = index // 2
        pos = index % 2
        up = jnp.where(pos == 0, low, 1 - low)
        dest = jnp.where(up == 1, n - 1 - s, s)

        @pl.when(s < (n + 1) // 2)
        def _():
            @pl.when(dest != me)
            def _():
                qkv_arrival(2, lax.rem(me - dest + n, n)).wait_recv()

            attend(dest)

            @pl.when(index == 0)
            def _():
                w_arrival(0).wait_recv()
                for chip in range(1, chips):
                    w_passed(chip).wait_recv()

        active = jnp.where(up == 1, jnp.where(me < dest, 1, 0), jnp.where(me > dest, 1, 0))
        inner = jnp.where(up == 1, jnp.where(me > 0, 1, 0), jnp.where(me < n - 1, 1, 0))

        for c in range(2):
            @pl.when(s < (n + 1) // 2)
            def _():
                project(dest, c)

            @pl.when(active == 1)
            def _():
                @pl.when(inner == 1)
                def _():
                    cut = slice(c * half, (c + 1) * half)
                    sum_arrival(dest, c).wait_recv()
                    part[dest, :, cut] = (part[dest, :, cut].astype(jnp.float32)
                                          + inbox[dest, :, cut].astype(jnp.float32)).astype(jnp.bfloat16)

                sum_copy(dest, up, c).start()

        return carry

    lax.fori_loop(0, 2 * n, item, 0)

    for c in range(2):
        cut = slice(c * half, (c + 1) * half)
        mine = part[me, :, cut].astype(jnp.float32)

        @pl.when(me > 0)
        def _():
            sum_arrival(me, c).wait_recv()

        @pl.when(me < n - 1)
        def _():
            sum_arrival(n, c).wait_recv()

        @pl.when(me == 0)
        def _():
            out[:, cut] = (mine + inbox[n, :, cut].astype(jnp.float32)).astype(jnp.bfloat16)

        @pl.when(me == n - 1)
        def _():
            out[:, cut] = (mine + inbox[me, :, cut].astype(jnp.float32)).astype(jnp.bfloat16)

        @pl.when((me > 0) & (me < n - 1))
        def _():
            out[:, cut] = (mine + inbox[me, :, cut].astype(jnp.float32)
                           + inbox[n, :, cut].astype(jnp.float32)).astype(jnp.bfloat16)

    for t in range(3):
        for off in range(1, n):
            qkv_copy(t, off).wait_send()
    for chip in range(chips):
        w_copy(chip).wait_send()
    for chip in range(1, chips):
        w_pass(chip).wait_send()

    def drain(dest, carry):
        @pl.when(dest != me)
        def _():
            for c in range(2):
                sum_copy(dest, jnp.where(dest > me, 1, 0), c).wait_send()
        return carry

    lax.fori_loop(0, n, drain, 0)


def per_device(n, m, queries, key_rows, value_rows, w_out):
    tokens, width = queries.shape[1:]
    depth, wcols = w_out.shape
    feats = width // n
    length = tokens * n
    dout = wcols * m
    bf16 = jnp.bfloat16
    vmem = pltpu.VMEM
    dma = pltpu.SemaphoreType.DMA
    flat = [a.reshape(tokens, width) for a in (queries, key_rows, value_rows)]
    result = pl.pallas_call(
        functools.partial(kernel, n, m),
        out_shape=jax.ShapeDtypeStruct((tokens, dout), bf16),
        in_specs=[pl.BlockSpec(memory_space=pl.ANY)] * 4,
        out_specs=pl.BlockSpec(memory_space=vmem),
        scratch_shapes=[
            vmem((length, feats), bf16), vmem((length, feats), bf16), vmem((length, feats), bf16),
            vmem((m, depth, wcols), bf16), vmem((tokens, feats), bf16),
            vmem((n, tokens, dout), bf16), vmem((n + 1, tokens, dout), bf16),
            dma((4,)), dma((3, n)), dma((3, n)), dma((m,)), dma((m,)), dma((n, 2)), dma((n + 1, 2)),
        ],
        compiler_params=pltpu.CompilerParams(
            collective_id=0, has_side_effects=True, vmem_limit_bytes=56 * 1024 * 1024),
        cost_estimate=pl.CostEstimate(
            flops=4 * length * length * feats + 2 * length * feats * dout,
            bytes_accessed=2 * (3 * tokens * width + depth * wcols),
            transcendentals=length * length * feats // HEAD_DIM),
    )(*flat, w_out)
    return result.reshape(1, tokens, dout)


def solution(mesh):
    n, m = mesh.shape["seq"], mesh.shape["dp"]
    in_specs = (P("dp", "seq", None), P("dp", "seq", None), P("dp", "seq", None), P("seq", "dp"))
    out_specs = P("dp", "seq", None)
    return jax.shard_map(
        functools.partial(per_device, n, m), mesh=mesh, in_specs=in_specs, out_specs=out_specs,
        check_vma=False
    )
```
